32 devices in a mesh: seq: 8 (over z, x), rep: 4 (over y, core).
Axes of the slice: x: 2, y: 2, z: 4, core: 2. Of those that a mesh axis runs over, the one named last changes fastest.
Arguments:
- hidden: bfloat16 [2, 512, 1024], P(None, 'seq'), may hold values from -6 to 6
- w_query: bfloat16 [1024, 1024], P(None, 'rep'), may hold values from -0.1875 to 0.1875
- w_key: bfloat16 [1024, 1024], P(None, 'rep'), may hold values from -0.4375 to 0.4375
- w_value: bfloat16 [1024, 1024], P(None, 'rep'), may hold values from -0.1875 to 0.1875
- w_out: bfloat16 [1024, 1024], P('rep'), may hold values from -0.1875 to 0.1875
- norm_gain: float32 [1024], P('rep'), may hold values from 0.1 to 1.9
- norm_bias: float32 [1024], P('rep'), may hold values from -3 to 3
- kv_cache: bfloat16 [8, 8704, 512], P('seq', None, 'rep'), may hold values from -300 to 300
- cache_lengths: int32 [2], replicated, may hold values from 1 to 8192, as said below
- append_counts: int32 [2], replicated, may hold values from 128 to 512, as said below
Outputs:
- out_hidden: bfloat16 [2, 512, 1024], P(None, 'seq', 'rep')
- new_entries: bfloat16 [8, 512, 512], P('seq', None, 'rep')
The draws below stay inside these ranges and needn't reach their ends.
Inputs may be any that keep to these rules, and one draw needn't show every extreme that they name: A request's cache holds its first cache_lengths entries; the most, 8192, is reached in every draw. `append_counts`: some request fills all 512 positions in every draw.
All inputs are finite; a program needn't handle non-finite values.
Results may differ from the reference program's by a relative error of at most 0.012.
The reference program's roundings to bfloat16 on the way count: a program that leaves them out, or rounds other values in their place, can miss the bound.
Values may be sent and summed in bfloat16 or wider, within the bound.
A program may use at most 64 MiB of HBM per device.

```python
import jax
import jax.numpy as jnp
from jax import lax

D = 1024
HEADS = 16
HD = 64
APPEND = 512
CACHE_MAX = 8192
REQ = 2
CAP = 8704
N_SEQ = 8
N_REP = 4


def draw_kv_cache(key, part):
    key_main = jax.random.fold_in(key, 0)
    shape_full = (N_SEQ, CAP, N_REP, 2, HD)
    normal_draw = jax.random.normal(key_main, shape_full, jnp.float32)
    key_part = normal_draw[:, :, :, 0:1] * 2.5
    value_part = normal_draw[:, :, :, 1:2]
    joined = jnp.clip(jnp.concatenate([key_part, value_part], axis=3), -300.0, 300.0)
    return joined.reshape(N_SEQ, CAP, N_REP * 2 * HD).astype(jnp.bfloat16)


def draw_cache_lengths(key, part):
    key_draw, key_pick = jax.random.split(key)
    tenant = jnp.arange(REQ, dtype=jnp.int32) % 4
    ceiling = CACHE_MAX * (tenant + 1) // 4
    raw_draw = jax.random.randint(key_draw, (REQ,), 0, CACHE_MAX, dtype=jnp.int32)
    lengths = 1 + raw_draw * ceiling // CACHE_MAX
    chosen = jax.random.randint(key_pick, (), 0, REQ, dtype=jnp.int32)
    return jnp.where(jnp.arange(REQ, dtype=jnp.int32) == chosen, CACHE_MAX, lengths).astype(jnp.int32)


def draw_append_counts(key, part):
    key_draw, key_pick = jax.random.split(key)
    counts = jax.random.randint(key_draw, (REQ,), APPEND // 4, APPEND + 1, dtype=jnp.int32)
    chosen = jax.random.randint(key_pick, (), 0, REQ, dtype=jnp.int32)
    return jnp.where(jnp.arange(REQ, dtype=jnp.int32) == chosen, APPEND, counts).astype(jnp.int32)


def levels(rng, shape, pieces, low, largest):
    def one(axis_at, blocks):
        draws = jax.random.uniform(jax.random.fold_in(jax.random.fold_in(rng, 6), axis_at), (blocks,), jnp.float32, low / len(pieces), largest / len(pieces))
        return jnp.repeat(jnp.exp(draws), shape[axis_at] // blocks).reshape((-1,) + (1,) * (len(shape) - axis_at - 1))

    gain = one(*pieces[0])
    for cut in pieces[1:]:
        gain = gain * one(*cut)
    return gain


def scatter_about(stream_key, dims, width, reach, shards=(), kind=jnp.bfloat16):
    drawn = width * jax.random.normal(stream_key, dims, jnp.float32)
    if shards:
        drawn = drawn * levels(stream_key, dims, shards, -0.22, 0.18)
    return jnp.clip(drawn, -reach, reach).astype(kind)


def setup_inputs(seed: int = 0) -> dict:
    keys = jax.random.split(jax.random.key(seed), 11)
    return {
        "hidden": scatter_about(keys[0], (REQ, APPEND, D), 1.0, 6.0, ((1, 8),)),
        "w_query": scatter_about(keys[1], (D, D), D ** -0.5, 0.1875, ((1, 4),)),
        "w_key": scatter_about(keys[2], (D, D), (D // 6) ** -0.5, 0.4375, ((1, 4),)),
        "w_value": scatter_about(keys[3], (D, D), D ** -0.5, 0.1875, ((1, 4),)),
        "w_out": scatter_about(keys[4], (D, D), D ** -0.5, 0.1875, ((0, 4),)),
        "norm_gain": jnp.clip(1.0 + 0.18 * jax.random.normal(keys[5], (D,), jnp.float32), 0.1, 1.9),
        "norm_bias": scatter_about(keys[6], (D,), 0.5, 3.0, ((0, 4),), jnp.float32),
        "kv_cache": draw_kv_cache(jax.random.fold_in(keys[10], 71), 0),
        "cache_lengths": draw_cache_lengths(jax.random.fold_in(keys[10], 71), 0),
        "append_counts": draw_append_counts(jax.random.fold_in(keys[10], 71), 0),
    }


def attend_one(items):
    queries, new_keys, new_values, cache_piece, cache_length, valid_count = items
    score_scale = HD ** (-0.5)
    key_rows = cache_piece[:, :HD]
    value_rows = cache_piece[:, HD:]
    cached_scores = jnp.dot(queries, key_rows.T, preferred_element_type=jnp.float32) * score_scale
    slot_ids = jnp.arange(CAP, dtype=jnp.int32)
    cached_scores = jnp.where(slot_ids[None, :] < cache_length, cached_scores, -jnp.inf)
    fresh_scores = jnp.dot(queries, new_keys.T, preferred_element_type=jnp.float32) * score_scale
    position_ids = jnp.arange(APPEND, dtype=jnp.int32)
    allowed = (position_ids[None, :] <= position_ids[:, None]) & (position_ids[None, :] < valid_count)
    fresh_scores = jnp.where(allowed, fresh_scores, -jnp.inf)
    row_max = jnp.maximum(cached_scores.max(axis=1), fresh_scores.max(axis=1))
    cached_exp = jnp.exp(cached_scores - row_max[:, None])
    fresh_exp = jnp.exp(fresh_scores - row_max[:, None])
    denominator = cached_exp.sum(axis=1) + fresh_exp.sum(axis=1)
    numerator = jnp.dot(cached_exp.astype(jnp.bfloat16), value_rows, preferred_element_type=jnp.float32)
    numerator = numerator + jnp.dot(fresh_exp.astype(jnp.bfloat16), new_values, preferred_element_type=jnp.float32)
    return (numerator / denominator[:, None]).astype(jnp.bfloat16)

def reference(hidden, w_query, w_key, w_value, w_out, norm_gain, norm_bias, kv_cache, cache_lengths, append_counts):
    group_size = HEADS // N_REP
    lanes_all = N_SEQ * N_REP
    flat_tokens = hidden.reshape(REQ * APPEND, D)

    def to_lanes(weight):
        projected = jnp.dot(flat_tokens, weight, preferred_element_type=jnp.float32).astype(jnp.bfloat16)
        projected = projected.reshape(REQ, APPEND, N_REP, group_size, HD).transpose(0, 3, 2, 1, 4)
        return projected.reshape(lanes_all, APPEND, HD)
    queries = to_lanes(w_query)
    new_keys = to_lanes(w_key)
    new_values = to_lanes(w_value)
    caches = kv_cache.reshape(N_SEQ, CAP, N_REP, 2 * HD).transpose(0, 2, 1, 3).reshape(lanes_all, CAP, 2 * HD)
    lane_request = jnp.arange(lanes_all, dtype=jnp.int32) // (N_REP * group_size)
    lane_lengths = cache_lengths[lane_request]
    lane_counts = append_counts[lane_request]
    attended = lax.map(attend_one, (queries, new_keys, new_values, caches, lane_lengths, lane_counts))
    valid_rows = jnp.arange(APPEND, dtype=jnp.int32)[None, :, None] < lane_counts[:, None, None]
    appended = jnp.concatenate([new_keys, new_values], axis=2)
    appended = jnp.where(valid_rows, appended, jnp.zeros_like(appended))
    new_entries = appended.reshape(N_SEQ, N_REP, APPEND, 2 * HD).transpose(0, 2, 1, 3).reshape(N_SEQ, APPEND, N_REP * 2 * HD)
    per_head = attended.reshape(REQ, group_size, N_REP, APPEND, HD)
    projection = jnp.zeros((REQ * APPEND, D), jnp.float32)
    for quarter in range(N_REP):
        head_block = per_head[:, :, quarter].transpose(0, 2, 1, 3).reshape(REQ * APPEND, group_size * HD)
        rows_used = w_out[quarter * group_size * HD:(quarter + 1) * group_size * HD]
        partial_sum = jnp.dot(head_block, rows_used, preferred_element_type=jnp.float32).astype(jnp.bfloat16)
        partial_sum = lax.optimization_barrier(partial_sum)
        projection = projection + partial_sum.astype(jnp.float32)
    combined = flat_tokens.astype(jnp.float32) + projection
    mean_row = combined.sum(axis=1) / D
    square_row = (combined * combined).sum(axis=1) / D
    variance = square_row - mean_row * mean_row
    normed = (combined - mean_row[:, None]) * lax.rsqrt(variance + 1e-05)[:, None] * norm_gain + norm_bias
    return (normed.astype(jnp.bfloat16).reshape(REQ, APPEND, D), new_entries)
```

```python
import functools

import jax
import jax.numpy as jnp
from jax import lax
from jax.experimental import pallas as pl
from jax.experimental.pallas import tpu as pltpu
from jax.sharding import PartitionSpec as P


def attend(queries, new_keys, new_values, cache_piece, cache_length, valid_count):
    head_size = queries.shape[1]
    score_scale = head_size ** (-0.5)
    row_count = queries.shape[0]
    contract_last = (((1,), (1,)), ((), ()))
    fresh_scores = (
        lax.dot_general(queries, new_keys, contract_last, preferred_element_type=jnp.float32)
        * score_scale
    )
    position_ids = jnp.arange(row_count, dtype=jnp.int32)
    allowed = (position_ids[None, :] <= position_ids[:, None]) & (
        position_ids[None, :] < valid_count
    )
    fresh_scores = jnp.where(allowed, fresh_scores, -jnp.inf)
    row_max = fresh_scores.max(axis=1)
    fresh_exp = jnp.exp(fresh_scores - row_max[:, None])
    denominator = fresh_exp.sum(axis=1)
    accumulated = jnp.dot(
        fresh_exp.astype(jnp.bfloat16), new_values, preferred_element_type=jnp.float32
    )
    block_size = min(512, cache_piece.shape[0])

    def visit_block(block_index, state_tuple):
        running_max, running_sum, running_acc = state_tuple
        cache_block = lax.dynamic_slice_in_dim(cache_piece, block_index * block_size, block_size, 0)
        block_scores = (
            lax.dot_general(
                queries,
                cache_block[:, :head_size],
                contract_last,
                preferred_element_type=jnp.float32,
            )
            * score_scale
        )
        slot_ids = block_index * block_size + jnp.arange(block_size, dtype=jnp.int32)
        block_scores = jnp.where(slot_ids[None, :] < cache_length, block_scores, -jnp.inf)
        newer_max = jnp.maximum(running_max, block_scores.max(axis=1))
        factor = jnp.exp(running_max - newer_max)
        block_exp = jnp.exp(block_scores - newer_max[:, None])
        gathered_values = jnp.dot(
            block_exp.astype(jnp.bfloat16),
            cache_block[:, head_size:],
            preferred_element_type=jnp.float32,
        )
        return (
            newer_max,
            running_sum * factor + block_exp.sum(axis=1),
            running_acc * factor[:, None] + gathered_values,
        )

    block_total = (cache_length + block_size - 1) // block_size
    row_max, denominator, accumulated = lax.fori_loop(
        0, block_total, visit_block, (row_max, denominator, accumulated)
    )
    return (accumulated / denominator[:, None]).astype(jnp.bfloat16)


def on_device(
    hidden,
    w_query,
    w_key,
    w_value,
    w_out,
    norm_gain,
    norm_bias,
    kv_cache,
    cache_lengths,
    append_counts,
):
    seq_count = lax.axis_size("seq")
    requests, positions, model_width = hidden.shape
    head_size = kv_cache.shape[2] // 2
    group_size = w_query.shape[1] // head_size
    append_len = positions * seq_count
    flat_tokens = hidden.reshape(requests * positions, model_width)

    def project(weight_part):
        return jnp.dot(flat_tokens, weight_part, preferred_element_type=jnp.float32).astype(
            jnp.bfloat16
        )

    stacked = jnp.stack([project(w_query), project(w_key), project(w_value)], axis=1)
    stacked = stacked.reshape(requests, positions, 3, group_size, head_size).transpose(
        0, 3, 2, 1, 4
    )
    outgoing = stacked.reshape(seq_count, 3, positions * head_size)
    incoming = lax.all_to_all(outgoing, "seq", split_axis=0, concat_axis=2, tiled=True)
    incoming = incoming.reshape(3, append_len, head_size)
    lane_number = lax.axis_index("seq")
    request_id = lane_number // group_size
    cache_length = cache_lengths[request_id]
    valid_count = append_counts[request_id]
    queries = incoming[0]
    new_keys = incoming[1]
    new_values = incoming[2]
    attended = attend(queries, new_keys, new_values, kv_cache[0], cache_length, valid_count)
    position_ids = jnp.arange(append_len, dtype=jnp.int32)
    appended = jnp.concatenate([new_keys, new_values], axis=1)
    appended = jnp.where((position_ids < valid_count)[:, None], appended, jnp.zeros_like(appended))[
        None
    ]
    returned = lax.all_to_all(
        attended.reshape(seq_count, positions * head_size),
        "seq",
        split_axis=0,
        concat_axis=0,
        tiled=True,
    )
    heads_local = returned.reshape(requests, group_size, positions, head_size).transpose(0, 2, 1, 3)
    heads_local = heads_local.reshape(requests * positions, group_size * head_size)
    partial_out = jnp.dot(heads_local, w_out, preferred_element_type=jnp.float32)
    rep_index = lax.axis_index("rep")
    share_width = norm_gain.shape[0]
    summed = lax.psum(partial_out.astype(jnp.bfloat16), "rep").astype(jnp.float32)
    combined = flat_tokens.astype(jnp.float32) + summed
    mean_row = combined.sum(axis=1) / model_width
    square_row = (combined * combined).sum(axis=1) / model_width
    combined = lax.dynamic_slice_in_dim(combined, rep_index * share_width, share_width, 1)
    variance = square_row - mean_row * mean_row
    normed = (combined - mean_row[:, None]) * lax.rsqrt(variance + 1e-05)[
        :, None
    ] * norm_gain + norm_bias
    return (normed.astype(jnp.bfloat16).reshape(requests, positions, share_width), appended)


MESH = pl.DeviceIdType.MESH
NEG = -1e30
KEY_ROWS = 1024
QUERY_ROWS = 128


def fused_kernel(
    seq_count,
    lengths_ref,
    counts_ref,
    hidden_hbm,
    wq_hbm,
    wk_hbm,
    wv_hbm,
    wo_hbm,
    gain_ref,
    bias_ref,
    kv_hbm,
    out_ref,
    entries_ref,
    hid,
    wq,
    wk,
    wv,
    wo,
    keys,
    values,
    scores,
    q_send,
    q_recv,
    kv_send,
    kv_recv,
    queries,
    new_values,
    ret_send,
    ret,
    heads,
    z_all,
    load_sem,
    q_ss,
    q_rs,
    kv_ss,
    kv_rs,
    wo_ss,
    wo_rs,
    ret_ss,
    ret_rs,
    pair_ss,
    pair_rs,
):
    bf16, f32 = jnp.bfloat16, jnp.float32
    lane = lax.axis_index("seq")
    rep = lax.axis_index("rep")
    far = lax.rem(rep + 2, 4)
    pair = rep + 1 - 2 * lax.rem(rep, 2)
    positions = hid.shape[0] // 2
    half = positions // 2
    width = hid.shape[1]
    share = wq.shape[1]
    append_len = queries.shape[0]
    cached = keys.shape[0]
    contract_last = (((1,), (1,)), ((), ()))

    def remote(src, dst, send, recv, to_seq, to_rep):
        return pltpu.make_async_remote_copy(
            src_ref=src,
            dst_ref=dst,
            send_sem=send,
            recv_sem=recv,
            device_id=(to_seq, to_rep),
            device_id_type=MESH,
        )

    barrier = pltpu.get_barrier_semaphore()
    for k in range(1, seq_count):
        pl.semaphore_signal(
            barrier, inc=1, device_id=(lax.rem(lane + k, seq_count), rep), device_id_type=MESH
        )
    for k in range(seq_count):
        pl.semaphore_signal(
            barrier, inc=1, device_id=(lax.rem(lane + k, seq_count), far), device_id_type=MESH
        )
    pl.semaphore_signal(barrier, inc=1, device_id=(lane, pair), device_id_type=MESH)

    loads = [
        pltpu.make_async_copy(hidden_hbm, hid, load_sem.at[0]),
        pltpu.make_async_copy(wq_hbm, wq, load_sem.at[1]),
        pltpu.make_async_copy(wk_hbm, wk, load_sem.at[2]),
        pltpu.make_async_copy(wv_hbm, wv, load_sem.at[3]),
        pltpu.make_async_copy(kv_hbm.at[0, pl.ds(0, cached)], keys, load_sem.at[4]),
        pltpu.make_async_copy(wo_hbm, wo.at[rep], load_sem.at[5]),
    ]
    for copy in loads:
        copy.start()

    loads[0].wait()
    loads[1].wait()
    q_all = jnp.dot(hid[...], wq[...], preferred_element_type=f32).astype(bf16).astype(f32)
    q_all = q_all * 0.125
    for dest in range(seq_count):
        r, i = dest // 4, dest % 4
        top = q_all[r * positions : r * positions + half, i * 64 : (i + 1) * 64]
        low = q_all[r * positions + half : (r + 1) * positions, i * 64 : (i + 1) * 64]
        q_send[dest] = jnp.concatenate([top, low], axis=1).astype(bf16)
    pl.semaphore_wait(barrier, 2 * seq_count)

    def q_copy(k):
        to = lax.rem(lane + k, seq_count)
        return remote(q_send.at[to], q_recv.at[lane], q_ss.at[k], q_rs.at[k], to, rep)

    for k in range(1, seq_count):
        q_copy(k).start()
    q_recv[lane] = q_send[lane]

    loads[2].wait()
    loads[3].wait()
    k_all = jnp.dot(hid[...], wk[...], preferred_element_type=f32)
    v_all = jnp.dot(hid[...], wv[...], preferred_element_type=f32)
    for dest in range(seq_count):
        r, i = dest // 4, dest % 4
        rows = slice(r * positions, (r + 1) * positions)
        cols = slice(i * 64, (i + 1) * 64)
        kv_send[dest] = jnp.concatenate([k_all[rows, cols], v_all[rows, cols]], axis=1).astype(bf16)

    def kv_copy(k):
        to = lax.rem(lane + k, seq_count)
        return remote(
            kv_send.at[to],
            kv_recv.at[lane],
            kv_ss.at[k],
            kv_rs.at[k],
            to,
            rep,
        )

    for k in range(1, seq_count):
        kv_copy(k).start()
    kv_recv[lane] = kv_send[lane]

    loads[5].wait()
    wo_far = remote(wo.at[rep], wo.at[rep], wo_ss.at[0], wo_rs.at[0], lane, far)
    wo_pair = remote(wo.at[rep], wo.at[rep], wo_ss.at[1], wo_rs.at[1], lane, pair)
    wo_pass = remote(wo.at[far], wo.at[far], wo_ss.at[2], wo_rs.at[2], lane, pair)
    wo_far.start()
    wo_pair.start()

    request = lane // 4
    length = lengths_ref[request]
    count = counts_ref[request]
    loads[4].wait()
    first = keys[0:16, :].astype(f32)[0:1, :]
    mask_rows = 256
    lanes = lax.broadcasted_iota(jnp.int32, (mask_rows, 128), 1)
    row_ids = lax.broadcasted_iota(jnp.int32, (mask_rows, 128), 0)

    def mask_block(b, carry):
        rows = pl.ds(pl.multiple_of(b * mask_rows, mask_rows), mask_rows)
        block = keys[rows, :].astype(f32)
        keep = row_ids + b * mask_rows < length
        keys[rows, :] = jnp.where(keep, block, first).astype(bf16)
        values[rows, :] = jnp.where(keep, jnp.where(lanes < 64, 1.0, block), 0.0).astype(bf16)
        return carry

    lax.fori_loop(0, cached // mask_rows, mask_block, 0)

    for k in range(1, seq_count):
        q_copy(k).wait_recv()
    lane_half = lax.broadcasted_iota(jnp.int32, (half, 128), 1) < 64
    for s in range(seq_count):
        both = q_recv[s].astype(f32)
        queries[s * positions : s * positions + half, :] = jnp.where(lane_half, both, 0.0).astype(bf16)
        queries[s * positions + half : (s + 1) * positions, :] = jnp.where(
            lane_half, pltpu.roll(both, 64, 1), 0.0
        ).astype(bf16)

    chunks = append_len // QUERY_ROWS
    per_chunk = QUERY_ROWS // positions
    own_chunk = lane // per_chunk

    for k in range(1, seq_count):
        kv_copy(k).wait_recv()
    lane_new = lax.broadcasted_iota(jnp.int32, (positions, 128), 1) < 64
    row_new = lax.broadcasted_iota(jnp.int32, (positions, 128), 0)
    for s in range(seq_count):
        block = kv_recv[s].astype(f32)
        new_values[s * positions : (s + 1) * positions, :] = jnp.where(lane_new, 1.0, block).astype(
            bf16
        )
        entries_ref[s * positions : (s + 1) * positions, :] = jnp.where(
            row_new + s * positions < count, block, 0.0
        ).astype(bf16)

    def ret_copy(side, s):
        to_rep = rep if side == 0 else far
        return remote(
            ret_send.at[s], ret.at[rep, lane], ret_ss.at[side, s], ret_rs.at[side, lane], s, to_rep
        )

    def visit_chunk(step, carry):
        chunk = lax.rem(own_chunk + 1 + step, chunks)
        start = pl.multiple_of(chunk * QUERY_ROWS, QUERY_ROWS)
        q = queries[pl.ds(start, QUERY_ROWS), :]
        fresh = lax.dot_general(
            q,
            kv_recv[...].reshape(append_len, 128),
            contract_last,
            preferred_element_type=f32,
        )
        col = lax.broadcasted_iota(jnp.int32, (QUERY_ROWS, append_len), 1)
        row = lax.broadcasted_iota(jnp.int32, (QUERY_ROWS, append_len), 0) + start
        fresh = jnp.where((col <= row) & (col < count), fresh, NEG)
        top = fresh.max(axis=1, keepdims=True)
        for b in range(cached // KEY_ROWS):
            rows = slice(b * KEY_ROWS, (b + 1) * KEY_ROWS)
            block = lax.dot_general(q, keys[rows, :], contract_last, preferred_element_type=f32)
            scores[:, rows] = block
            top = jnp.maximum(top, block.max(axis=1, keepdims=True))
        total = jnp.dot(
            jnp.exp(fresh - top).astype(bf16), new_values[...], preferred_element_type=f32
        )
        for b in range(cached // KEY_ROWS):
            rows = slice(b * KEY_ROWS, (b + 1) * KEY_ROWS)
            weight = jnp.exp(scores[:, rows] - top).astype(bf16)
            total = total + jnp.dot(weight, values[rows, :], preferred_element_type=f32)
        attn = total / pltpu.roll(total, 64, 1)
        for t in range(per_chunk):
            a = attn[t * positions : t * positions + half, :]
            b = attn[t * positions + half : (t + 1) * positions, :]
            s = chunk * per_chunk + t
            ret_send[s] = jnp.where(lane_half, pltpu.roll(a, 64, 1), b).astype(bf16)
            ret_copy(1, s).start()

            @pl.when(s != lane)
            def _():
                ret_copy(0, s).start()

            @pl.when(s == lane)
            def _():
                ret[rep, lane] = ret_send[s]

        return carry

    lax.fori_loop(0, chunks, visit_chunk, 0)

    wo_far.wait_recv()
    wo_pass.start()

    for k in range(seq_count):
        s = lax.rem(lane + k, seq_count)
        remote(
            ret_send.at[s], ret.at[far, s], ret_ss.at[1, s], ret_rs.at[1, s], s, far
        ).wait_recv()
    far_pair = remote(ret.at[far], ret.at[far], pair_ss.at[1], pair_rs.at[1], lane, pair)
    far_pair.start()
    for k in range(1, seq_count):
        s = lax.rem(lane + k, seq_count)
        remote(
            ret_send.at[s], ret.at[rep, s], ret_ss.at[0, s], ret_rs.at[0, s], s, rep
        ).wait_recv()
    own_pair = remote(ret.at[rep], ret.at[rep], pair_ss.at[0], pair_rs.at[0], lane, pair)
    own_pair.start()

    def project(which):
        for r in range(2):
            parts = [ret[which, r * 4 + i].astype(f32) for i in range(4)]
            upper = [jnp.where(lane_half, parts[2 * g], pltpu.roll(parts[2 * g + 1], 64, 1)) for g in range(2)]
            lower = [jnp.where(lane_half, pltpu.roll(parts[2 * g], 64, 1), parts[2 * g + 1]) for g in range(2)]
            for g in range(2):
                cols = slice(g * 128, (g + 1) * 128)
                heads[r * positions : r * positions + half, cols] = upper[g].astype(bf16)
                heads[r * positions + half : (r + 1) * positions, cols] = lower[g].astype(bf16)
        part = jnp.dot(heads[...], wo[which], preferred_element_type=f32)
        return part.astype(bf16).astype(f32)

    z_all[...] = hid[...].astype(f32) + project(rep)
    z_all[...] += project(far)
    wo_pair.wait_recv()
    wo_pass.wait_recv()
    own_pair.wait_recv()
    z_all[...] += project(pair)
    far_pair.wait_recv()
    z_all[...] += project(lax.rem(pair + 2, 4))
    z = z_all[...]
    mean = z.sum(axis=1, keepdims=True) / width
    square = (z * z).sum(axis=1, keepdims=True) / width
    mine = z_all[:, pl.ds(pl.multiple_of(rep * share, share), share)]
    scale = lax.rsqrt(square - mean * mean + 1e-05)
    out_ref[...] = ((mine - mean) * scale * gain_ref[...] + bias_ref[...]).astype(bf16)

    for k in range(1, seq_count):
        q_copy(k).wait_send()
        kv_copy(k).wait_send()
    for k in range(seq_count):
        s = lax.rem(lane + k, seq_count)
        ret_copy(1, s).wait_send()
        if k:
            ret_copy(0, s).wait_send()
    for copy in (wo_far, wo_pair, wo_pass, own_pair, far_pair):
        copy.wait_send()


def fused(
    hidden,
    w_query,
    w_key,
    w_value,
    w_out,
    norm_gain,
    norm_bias,
    kv_cache,
    cache_lengths,
    append_counts,
):
    seq_count = lax.axis_size("seq")
    requests, positions, width = hidden.shape
    share = w_query.shape[1]
    tokens = requests * positions
    append_len = positions * seq_count
    cached = kv_cache.shape[1] - append_len
    bf16, f32 = jnp.bfloat16, jnp.float32
    any_spec = pl.BlockSpec(memory_space=pl.ANY)
    vmem_spec = pl.BlockSpec(memory_space=pltpu.VMEM)
    smem_spec = pl.BlockSpec(memory_space=pltpu.SMEM)
    dma = pltpu.SemaphoreType.DMA
    half = positions // 2
    out, entries = pl.pallas_call(
        functools.partial(fused_kernel, seq_count),
        out_shape=(
            jax.ShapeDtypeStruct((tokens, share), bf16),
            jax.ShapeDtypeStruct((append_len, 128), bf16),
        ),
        in_specs=[smem_spec] * 2 + [any_spec] * 5 + [vmem_spec] * 2 + [any_spec],
        out_specs=(vmem_spec, vmem_spec),
        scratch_shapes=[
            pltpu.VMEM((tokens, width), bf16),
            pltpu.VMEM((width, share), bf16),
            pltpu.VMEM((width, share), bf16),
            pltpu.VMEM((width, share), bf16),
            pltpu.VMEM((4, share, width), bf16),
            pltpu.VMEM((cached, 128), bf16),
            pltpu.VMEM((cached, 128), bf16),
            pltpu.VMEM((QUERY_ROWS, cached), f32),
            pltpu.VMEM((seq_count, half, 128), bf16),
            pltpu.VMEM((seq_count, half, 128), bf16),
            pltpu.VMEM((seq_count, positions, 128), bf16),
            pltpu.VMEM((seq_count, positions, 128), bf16),
            pltpu.VMEM((append_len, 128), bf16),
            pltpu.VMEM((append_len, 128), bf16),
            pltpu.VMEM((seq_count, half, 128), bf16),
            pltpu.VMEM((4, seq_count, half, 128), bf16),
            pltpu.VMEM((tokens, share), bf16),
            pltpu.VMEM((tokens, width), f32),
            dma((6,)),
            dma((seq_count,)),
            dma((seq_count,)),
            dma((seq_count,)),
            dma((seq_count,)),
            dma((3,)),
            dma((3,)),
            dma((2, seq_count)),
            dma((2, seq_count)),
            dma((2,)),
            dma((2,)),
        ],
        compiler_params=pltpu.CompilerParams(
            collective_id=0, has_side_effects=True, vmem_limit_bytes=40 * 1024 * 1024
        ),
        name="sublayer",
    )(
        cache_lengths,
        append_counts,
        hidden.reshape(tokens, width),
        w_query,
        w_key,
        w_value,
        w_out,
        norm_gain.reshape(1, share),
        norm_bias.reshape(1, share),
        kv_cache,
    )
    return out.reshape(requests, positions, share), entries[None]


def solution(mesh):
    fits = mesh.shape["seq"] == 8 and mesh.shape["rep"] == 4
    return jax.shard_map(
        fused if fits else on_device,
        mesh=mesh,
        in_specs=(
            P(None, "seq", None),
            P(None, "rep"),
            P(None, "rep"),
            P(None, "rep"),
            P("rep", None),
            P("rep"),
            P("rep"),
            P("seq", None, "rep"),
            P(),
            P(),
        ),
        out_specs=(P(None, "seq", "rep"), P("seq", None, "rep")),
        check_vma=False,
    )
```

```python
import functools

import jax
import jax.numpy as jnp
from jax import lax
from jax.experimental import pallas as pl
from jax.experimental.pallas import tpu as pltpu
from jax.sharding import PartitionSpec as P


def attend(queries, new_keys, new_values, cache_piece, cache_length, valid_count):
    head_size = queries.shape[1]
    score_scale = head_size ** (-0.5)
    row_count = queries.shape[0]
    contract_last = (((1,), (1,)), ((), ()))
    fresh_scores = (
        lax.dot_general(queries, new_keys, contract_last, preferred_element_type=jnp.float32)
        * score_scale
    )
    position_ids = jnp.arange(row_count, dtype=jnp.int32)
    allowed = (position_ids[None, :] <= position_ids[:, None]) & (
        position_ids[None, :] < valid_count
    )
    fresh_scores = jnp.where(allowed, fresh_scores, -jnp.inf)
    row_max = fresh_scores.max(axis=1)
    fresh_exp = jnp.exp(fresh_scores - row_max[:, None])
    denominator = fresh_exp.sum(axis=1)
    accumulated = jnp.dot(
        fresh_exp.astype(jnp.bfloat16), new_values, preferred_element_type=jnp.float32
    )
    block_size = min(512, cache_piece.shape[0])

    def visit_block(block_index, state_tuple):
        running_max, running_sum, running_acc = state_tuple
        cache_block = lax.dynamic_slice_in_dim(cache_piece, block_index * block_size, block_size, 0)
        block_scores = (
            lax.dot_general(
                queries,
                cache_block[:, :head_size],
                contract_last,
                preferred_element_type=jnp.float32,
            )
            * score_scale
        )
        slot_ids = block_index * block_size + jnp.arange(block_size, dtype=jnp.int32)
        block_scores = jnp.where(slot_ids[None, :] < cache_length, block_scores, -jnp.inf)
        newer_max = jnp.maximum(running_max, block_scores.max(axis=1))
        factor = jnp.exp(running_max - newer_max)
        block_exp = jnp.exp(block_scores - newer_max[:, None])
        gathered_values = jnp.dot(
            block_exp.astype(jnp.bfloat16),
            cache_block[:, head_size:],
            preferred_element_type=jnp.float32,
        )
        return (
            newer_max,
            running_sum * factor + block_exp.sum(axis=1),
            running_acc * factor[:, None] + gathered_values,
        )

    block_total = (cache_length + block_size - 1) // block_size
    row_max, denominator, accumulated = lax.fori_loop(
        0, block_total, visit_block, (row_max, denominator, accumulated)
    )
    return (accumulated / denominator[:, None]).astype(jnp.bfloat16)


def on_device(
    hidden,
    w_query,
    w_key,
    w_value,
    w_out,
    norm_gain,
    norm_bias,
    kv_cache,
    cache_lengths,
    append_counts,
):
    seq_count = lax.axis_size("seq")
    requests, positions, model_width = hidden.shape
    head_size = kv_cache.shape[2] // 2
    group_size = w_query.shape[1] // head_size
    append_len = positions * seq_count
    flat_tokens = hidden.reshape(requests * positions, model_width)

    def project(weight_part):
        return jnp.dot(flat_tokens, weight_part, preferred_element_type=jnp.float32).astype(
            jnp.bfloat16
        )

    stacked = jnp.stack([project(w_query), project(w_key), project(w_value)], axis=1)
    stacked = stacked.reshape(requests, positions, 3, group_size, head_size).transpose(
        0, 3, 2, 1, 4
    )
    outgoing = stacked.reshape(seq_count, 3, positions * head_size)
    incoming = lax.all_to_all(outgoing, "seq", split_axis=0, concat_axis=2, tiled=True)
    incoming = incoming.reshape(3, append_len, head_size)
    lane_number = lax.axis_index("seq")
    request_id = lane_number // group_size
    cache_length = cache_lengths[request_id]
    valid_count = append_counts[request_id]
    queries = incoming[0]
    new_keys = incoming[1]
    new_values = incoming[2]
    attended = attend(queries, new_keys, new_values, kv_cache[0], cache_length, valid_count)
    position_ids = jnp.arange(append_len, dtype=jnp.int32)
    appended = jnp.concatenate([new_keys, new_values], axis=1)
    appended = jnp.where((position_ids < valid_count)[:, None], appended, jnp.zeros_like(appended))[
        None
    ]
    returned = lax.all_to_all(
        attended.reshape(seq_count, positions * head_size),
        "seq",
        split_axis=0,
        concat_axis=0,
        tiled=True,
    )
    heads_local = returned.reshape(requests, group_size, positions, head_size).transpose(0, 2, 1, 3)
    heads_local = heads_local.reshape(requests * positions, group_size * head_size)
    partial_out = jnp.dot(heads_local, w_out, preferred_element_type=jnp.float32)
    rep_index = lax.axis_index("rep")
    share_width = norm_gain.shape[0]
    summed = lax.psum(partial_out.astype(jnp.bfloat16), "rep").astype(jnp.float32)
    combined = flat_tokens.astype(jnp.float32) + summed
    mean_row = combined.sum(axis=1) / model_width
    square_row = (combined * combined).sum(axis=1) / model_width
    combined = lax.dynamic_slice_in_dim(combined, rep_index * share_width, share_width, 1)
    variance = square_row - mean_row * mean_row
    normed = (combined - mean_row[:, None]) * lax.rsqrt(variance + 1e-05)[
        :, None
    ] * norm_gain + norm_bias
    return (normed.astype(jnp.bfloat16).reshape(requests, positions, share_width), appended)


MESH = pl.DeviceIdType.MESH
NEG = -1e30
KEY_ROWS = 1024
QUERY_ROWS = 256


def fused_kernel(
    seq_count,
    lengths_ref,
    counts_ref,
    hidden_hbm,
    wq_hbm,
    wk_hbm,
    wv_hbm,
    wo_hbm,
    gain_ref,
    bias_ref,
    kv_hbm,
    out_ref,
    entries_ref,
    hid,
    wq,
    wk,
    wv,
    wo,
    keys,
    values,
    q_send,
    q_recv,
    kv_send,
    kv_recv,
    queries,
    new_values,
    ret_send,
    ret,
    heads,
    z_all,
    load_sem,
    q_ss,
    q_rs,
    kv_ss,
    kv_rs,
    wo_ss,
    wo_rs,
    ret_ss,
    ret_rs,
    pair_ss,
    pair_rs,
):
    bf16, f32 = jnp.bfloat16, jnp.float32
    lane = lax.axis_index("seq")
    rep = lax.axis_index("rep")
    far = lax.rem(rep + 2, 4)
    pair = rep + 1 - 2 * lax.rem(rep, 2)
    cross = lax.rem(pair + 2, 4)
    near_lanes = seq_count // 2
    near_base = lane // near_lanes * near_lanes
    away_base = near_lanes - near_base
    positions = hid.shape[0] // 2
    half = positions // 2
    width = hid.shape[1]
    share = wq.shape[1]
    append_len = queries.shape[0]
    cached = keys.shape[0]
    contract_last = (((1,), (1,)), ((), ()))

    def remote(src, dst, send, recv, to_seq, to_rep):
        return pltpu.make_async_remote_copy(
            src_ref=src,
            dst_ref=dst,
            send_sem=send,
            recv_sem=recv,
            device_id=(to_seq, to_rep),
            device_id_type=MESH,
        )

    loads = [
        pltpu.make_async_copy(hidden_hbm, hid, load_sem.at[0]),
        pltpu.make_async_copy(wq_hbm, wq, load_sem.at[1]),
        pltpu.make_async_copy(wk_hbm, wk, load_sem.at[2]),
        pltpu.make_async_copy(wv_hbm, wv, load_sem.at[3]),
        pltpu.make_async_copy(kv_hbm.at[0, pl.ds(0, cached)], keys, load_sem.at[4]),
        pltpu.make_async_copy(wo_hbm, wo.at[rep], load_sem.at[5]),
    ]
    for copy in loads:
        copy.start()

    barrier = pltpu.get_barrier_semaphore()
    for k in range(1, seq_count):
        pl.semaphore_signal(
            barrier, inc=1, device_id=(lax.rem(lane + k, seq_count), rep), device_id_type=MESH
        )
    for k in range(seq_count):
        pl.semaphore_signal(
            barrier, inc=1, device_id=(lax.rem(lane + k, seq_count), far), device_id_type=MESH
        )
    for k in range(near_lanes):
        for to in (pair, cross):
            pl.semaphore_signal(
                barrier,
                inc=1,
                device_id=(near_base + lax.rem(lane + k, near_lanes), to),
                device_id_type=MESH,
            )

    wo_far = remote(wo_hbm, wo.at[rep], wo_ss.at[0], wo_rs.at[0], lane, far)
    wo_pair = remote(wo_hbm, wo.at[rep], wo_ss.at[1], wo_rs.at[1], lane, pair)
    wo_pass = remote(wo.at[far], wo.at[far], wo_ss.at[2], wo_rs.at[2], lane, pair)
    pl.semaphore_wait(barrier, 3 * seq_count - 1)
    wo_far.start()

    loads[0].wait()
    loads[1].wait()
    q_all = jnp.dot(hid[...], wq[...], preferred_element_type=f32).astype(bf16).astype(f32)
    q_all = q_all * 0.125
    for dest in range(seq_count):
        r, i = dest // 4, dest % 4
        top = q_all[r * positions : r * positions + half, i * 64 : (i + 1) * 64]
        low = q_all[r * positions + half : (r + 1) * positions, i * 64 : (i + 1) * 64]
        q_send[dest] = jnp.concatenate([top, low], axis=1).astype(bf16)

    def q_copy(k):
        to = lax.rem(lane + k, seq_count)
        return remote(q_send.at[to], q_recv.at[lane], q_ss.at[k], q_rs.at[k], to, rep)

    for k in range(1, seq_count):
        q_copy(k).start()
    q_recv[lane] = q_send[lane]

    loads[2].wait()
    loads[3].wait()
    k_all = jnp.dot(hid[...], wk[...], preferred_element_type=f32)
    v_all = jnp.dot(hid[...], wv[...], preferred_element_type=f32)
    for dest in range(seq_count):
        r, i = dest // 4, dest % 4
        rows = slice(r * positions, (r + 1) * positions)
        cols = slice(i * 64, (i + 1) * 64)
        kv_send[dest] = jnp.concatenate([k_all[rows, cols], v_all[rows, cols]], axis=1).astype(bf16)

    def kv_copy(k):
        to = lax.rem(lane + k, seq_count)
        return remote(
            kv_send.at[to],
            kv_recv.at[lane],
            kv_ss.at[k],
            kv_rs.at[k],
            to,
            rep,
        )

    for k in range(1, seq_count):
        kv_copy(k).start()
    kv_recv[lane] = kv_send[lane]

    wo_pair.start()

    request = lane // 4
    length = lengths_ref[request]
    count = counts_ref[request]
    loads[4].wait()
    first = keys[0:16, :].astype(f32)[0:1, :]
    mask_rows = 256
    lanes = lax.broadcasted_iota(jnp.int32, (mask_rows, 128), 1)
    row_ids = lax.broadcasted_iota(jnp.int32, (mask_rows, 128), 0)

    def mask_block(b, carry):
        rows = pl.ds(pl.multiple_of(b * mask_rows, mask_rows), mask_rows)
        block = keys[rows, :].astype(f32)
        keep = row_ids + b * mask_rows < length
        keys[rows, :] = jnp.where(keep, block, first).astype(bf16)
        values[rows, :] = jnp.where(keep, jnp.where(lanes < 64, 1.0, block), 0.0).astype(bf16)
        return carry

    lax.fori_loop(0, cached // mask_rows, mask_block, 0)

    for k in range(1, seq_count):
        q_copy(k).wait_recv()
    lane_half = lax.broadcasted_iota(jnp.int32, (half, 128), 1) < 64
    for s in range(seq_count):
        both = q_recv[s].astype(f32)
        queries[s * positions : s * positions + half, :] = jnp.where(lane_half, both, 0.0).astype(bf16)
        queries[s * positions + half : (s + 1) * positions, :] = jnp.where(
            lane_half, pltpu.roll(both, 64, 1), 0.0
        ).astype(bf16)

    per_chunk = QUERY_ROWS // positions
    own_chunk = lane // per_chunk
    lane_new = lax.broadcasted_iota(jnp.int32, (positions, 128), 1) < 64
    row_new = lax.broadcasted_iota(jnp.int32, (positions, 128), 0)

    def take_new_entries():
        for k in range(1, seq_count):
            kv_copy(k).wait_recv()
        for s in range(seq_count):
            block = kv_recv[s].astype(f32)
            rows = slice(s * positions, (s + 1) * positions)
            new_values[rows, :] = jnp.where(lane_new, 1.0, block).astype(bf16)
            entries_ref[rows, :] = jnp.where(
                row_new + s * positions < count, block, 0.0
            ).astype(bf16)

    to_reps = (rep, far, pair, cross)

    def ret_copy(side, s):
        return remote(
            ret_send.at[s],
            ret.at[rep, lane],
            ret_ss.at[side, s],
            ret_rs.at[side, lane],
            s,
            to_reps[side],
        )

    def wait_ret(side, s):
        remote(
            ret_send.at[s],
            ret.at[to_reps[side], s],
            ret_ss.at[side, s],
            ret_rs.at[side, s],
            s,
            to_reps[side],
        ).wait_recv()

    blocks = cached // KEY_ROWS
    for step in range(2):
        chunk = 1 - own_chunk if step == 0 else own_chunk
        start = pl.multiple_of(chunk * QUERY_ROWS, QUERY_ROWS)
        q = queries[pl.ds(start, QUERY_ROWS), :]

        def block_scores(b):
            if b < blocks:
                block = keys[b * KEY_ROWS : (b + 1) * KEY_ROWS, :]
                return lax.dot_general(q, block, contract_last, preferred_element_type=f32)
            fresh = kv_recv[...].reshape(append_len, 128)
            fresh = lax.dot_general(q, fresh, contract_last, preferred_element_type=f32)
            col = lax.broadcasted_iota(jnp.int32, (QUERY_ROWS, append_len), 1)
            row = lax.broadcasted_iota(jnp.int32, (QUERY_ROWS, append_len), 0) + start
            return jnp.where((col <= row) & (col < count), fresh, NEG)

        current = block_scores(0)
        top = total = None
        for b in range(blocks + 1):
            following = None
            if b < blocks:
                if step == 0 and b == blocks - 1:
                    take_new_entries()
                following = block_scores(b + 1)
            newer = current.max(axis=1, keepdims=True)
            if b > 0:
                newer = jnp.maximum(top, newer)
            weight = jnp.exp(current - newer).astype(bf16)
            rows = values[b * KEY_ROWS : (b + 1) * KEY_ROWS, :] if b < blocks else new_values[...]
            part = jnp.dot(weight, rows, preferred_element_type=f32)
            total = part if b == 0 else total * jnp.exp(top - newer) + part
            top, current = newer, following
        attn = total / pltpu.roll(total, 64, 1)
        for t in range(per_chunk):
            upper = attn[t * positions : t * positions + half, :]
            lower = attn[t * positions + half : (t + 1) * positions, :]
            s = chunk * per_chunk + t
            ret_send[s] = jnp.where(lane_half, pltpu.roll(upper, 64, 1), lower).astype(bf16)
            if step == 0:
                ret_copy(0, s).start()
                ret_copy(1, s).start()
        if step == 1:
            for k in range(near_lanes):
                s = near_base + lax.rem(lane + k, near_lanes)
                for side in range(4):
                    if k or side:
                        ret_copy(side, s).start()
            ret[rep, lane] = ret_send[lane]

    wo_far.wait_recv()
    wo_pass.start()

    passes = []
    for side in (0, 1):
        for k in range(near_lanes):
            wait_ret(side, away_base + k)
        away = ret.at[to_reps[side], pl.ds(away_base, near_lanes)]
        passes.append(remote(away, away, pair_ss.at[side], pair_rs.at[side], lane, pair))
        passes[side].start()
    for k in range(near_lanes):
        for side in range(4):
            if k or side:
                wait_ret(side, near_base + lax.rem(lane + k, near_lanes))

    def project(which):
        for r in range(2):
            parts = [ret[which, r * 4 + i].astype(f32) for i in range(4)]
            upper = [jnp.where(lane_half, parts[2 * g], pltpu.roll(parts[2 * g + 1], 64, 1)) for g in range(2)]
            lower = [jnp.where(lane_half, pltpu.roll(parts[2 * g], 64, 1), parts[2 * g + 1]) for g in range(2)]
            for g in range(2):
                cols = slice(g * 128, (g + 1) * 128)
                heads[r * positions : r * positions + half, cols] = upper[g].astype(bf16)
                heads[r * positions + half : (r + 1) * positions, cols] = lower[g].astype(bf16)
        part = jnp.dot(heads[...], wo[which], preferred_element_type=f32)
        return part.astype(bf16).astype(f32)

    loads[5].wait()
    z_all[...] = hid[...].astype(f32) + project(rep)
    z_all[...] += project(far)
    wo_pair.wait_recv()
    passes[0].wait_recv()
    z_all[...] += project(pair)
    wo_pass.wait_recv()
    passes[1].wait_recv()
    z_all[...] += project(cross)
    z = z_all[...]
    mean = z.sum(axis=1, keepdims=True) / width
    square = (z * z).sum(axis=1, keepdims=True) / width
    mine = z_all[:, pl.ds(pl.multiple_of(rep * share, share), share)]
    scale = lax.rsqrt(square - mean * mean + 1e-05)
    out_ref[...] = ((mine - mean) * scale * gain_ref[...] + bias_ref[...]).astype(bf16)

    for k in range(1, seq_count):
        q_copy(k).wait_send()
        kv_copy(k).wait_send()
    for k in range(near_lanes):
        for side in range(4):
            if side < 2:
                ret_copy(side, away_base + k).wait_send()
            if k or side:
                ret_copy(side, near_base + lax.rem(lane + k, near_lanes)).wait_send()
    for copy in [wo_far, wo_pair, wo_pass] + passes:
        copy.wait_send()


def fused(
    hidden,
    w_query,
    w_key,
    w_value,
    w_out,
    norm_gain,
    norm_bias,
    kv_cache,
    cache_lengths,
    append_counts,
):
    seq_count = lax.axis_size("seq")
    requests, positions, width = hidden.shape
    share = w_query.shape[1]
    tokens = requests * positions
    append_len = positions * seq_count
    cached = kv_cache.shape[1] - append_len
    bf16, f32 = jnp.bfloat16, jnp.float32
    any_spec = pl.BlockSpec(memory_space=pltpu.HBM)
    vmem_spec = pl.BlockSpec(memory_space=pltpu.VMEM)
    smem_spec = pl.BlockSpec(memory_space=pltpu.SMEM)
    dma = pltpu.SemaphoreType.DMA
    half = positions // 2
    out, entries = pl.pallas_call(
        functools.partial(fused_kernel, seq_count),
        out_shape=(
            jax.ShapeDtypeStruct((tokens, share), bf16),
            jax.ShapeDtypeStruct((append_len, 128), bf16),
        ),
        in_specs=[smem_spec] * 2 + [any_spec] * 5 + [vmem_spec] * 2 + [any_spec],
        out_specs=(vmem_spec, vmem_spec),
        scratch_shapes=[
            pltpu.VMEM((tokens, width), bf16),
            pltpu.VMEM((width, share), bf16),
            pltpu.VMEM((width, share), bf16),
            pltpu.VMEM((width, share), bf16),
            pltpu.VMEM((4, share, width), bf16),
            pltpu.VMEM((cached, 128), bf16),
            pltpu.VMEM((cached, 128), bf16),
            pltpu.VMEM((seq_count, half, 128), bf16),
            pltpu.VMEM((seq_count, half, 128), bf16),
            pltpu.VMEM((seq_count, positions, 128), bf16),
            pltpu.VMEM((seq_count, positions, 128), bf16),
            pltpu.VMEM((append_len, 128), bf16),
            pltpu.VMEM((append_len, 128), bf16),
            pltpu.VMEM((seq_count, half, 128), bf16),
            pltpu.VMEM((4, seq_count, half, 128), bf16),
            pltpu.VMEM((tokens, share), bf16),
            pltpu.VMEM((tokens, width), f32),
            dma((6,)),
            dma((seq_count,)),
            dma((seq_count,)),
            dma((seq_count,)),
            dma((seq_count,)),
            dma((3,)),
            dma((3,)),
            dma((4, seq_count)),
            dma((4, seq_count)),
            dma((2,)),
            dma((2,)),
        ],
        compiler_params=pltpu.CompilerParams(
            collective_id=0, has_side_effects=True, vmem_limit_bytes=63 * 1024 * 1024
        ),
        name="sublayer",
    )(
        cache_lengths,
        append_counts,
        hidden.reshape(tokens, width),
        w_query,
        w_key,
        w_value,
        w_out,
        norm_gain.reshape(1, share),
        norm_bias.reshape(1, share),
        kv_cache,
    )
    return out.reshape(requests, positions, share), entries[None]


def solution(mesh):
    fits = mesh.shape["seq"] == 8 and mesh.shape["rep"] == 4
    return jax.shard_map(
        fused if fits else on_device,
        mesh=mesh,
        in_specs=(
            P(None, "seq", None),
            P(None, "rep"),
            P(None, "rep"),
            P(None, "rep"),
            P("rep", None),
            P("rep"),
            P("rep"),
            P("seq", None, "rep"),
            P(),
            P(),
        ),
        out_specs=(P(None, "seq", "rep"), P("seq", None, "rep")),
        check_vma=False,
    )
```

```python
import functools

import jax
import jax.numpy as jnp
from jax import lax
from jax.experimental import pallas as pl
from jax.experimental.pallas import tpu as pltpu
from jax.sharding import PartitionSpec as P


def attend(queries, new_keys, new_values, cache_piece, cache_length, valid_count):
    head_size = queries.shape[1]
    score_scale = head_size ** (-0.5)
    row_count = queries.shape[0]
    contract_last = (((1,), (1,)), ((), ()))
    fresh_scores = (
        lax.dot_general(queries, new_keys, contract_last, preferred_element_type=jnp.float32)
        * score_scale
    )
    position_ids = jnp.arange(row_count, dtype=jnp.int32)
    allowed = (position_ids[None, :] <= position_ids[:, None]) & (
        position_ids[None, :] < valid_count
    )
    fresh_scores = jnp.where(allowed, fresh_scores, -jnp.inf)
    row_max = fresh_scores.max(axis=1)
    fresh_exp = jnp.exp(fresh_scores - row_max[:, None])
    denominator = fresh_exp.sum(axis=1)
    accumulated = jnp.dot(
        fresh_exp.astype(jnp.bfloat16), new_values, preferred_element_type=jnp.float32
    )
    block_size = min(512, cache_piece.shape[0])

    def visit_block(block_index, state_tuple):
        running_max, running_sum, running_acc = state_tuple
        cache_block = lax.dynamic_slice_in_dim(cache_piece, block_index * block_size, block_size, 0)
        block_scores = (
            lax.dot_general(
                queries,
                cache_block[:, :head_size],
                contract_last,
                preferred_element_type=jnp.float32,
            )
            * score_scale
        )
        slot_ids = block_index * block_size + jnp.arange(block_size, dtype=jnp.int32)
        block_scores = jnp.where(slot_ids[None, :] < cache_length, block_scores, -jnp.inf)
        newer_max = jnp.maximum(running_max, block_scores.max(axis=1))
        factor = jnp.exp(running_max - newer_max)
        block_exp = jnp.exp(block_scores - newer_max[:, None])
        gathered_values = jnp.dot(
            block_exp.astype(jnp.bfloat16),
            cache_block[:, head_size:],
            preferred_element_type=jnp.float32,
        )
        return (
            newer_max,
            running_sum * factor + block_exp.sum(axis=1),
            running_acc * factor[:, None] + gathered_values,
        )

    block_total = (cache_length + block_size - 1) // block_size
    row_max, denominator, accumulated = lax.fori_loop(
        0, block_total, visit_block, (row_max, denominator, accumulated)
    )
    return (accumulated / denominator[:, None]).astype(jnp.bfloat16)


def on_device(
    hidden,
    w_query,
    w_key,
    w_value,
    w_out,
    norm_gain,
    norm_bias,
    kv_cache,
    cache_lengths,
    append_counts,
):
    seq_count = lax.axis_size("seq")
    requests, positions, model_width = hidden.shape
    head_size = kv_cache.shape[2] // 2
    group_size = w_query.shape[1] // head_size
    append_len = positions * seq_count
    flat_tokens = hidden.reshape(requests * positions, model_width)

    def project(weight_part):
        return jnp.dot(flat_tokens, weight_part, preferred_element_type=jnp.float32).astype(
            jnp.bfloat16
        )

    stacked = jnp.stack([project(w_query), project(w_key), project(w_value)], axis=1)
    stacked = stacked.reshape(requests, positions, 3, group_size, head_size).transpose(
        0, 3, 2, 1, 4
    )
    outgoing = stacked.reshape(seq_count, 3, positions * head_size)
    incoming = lax.all_to_all(outgoing, "seq", split_axis=0, concat_axis=2, tiled=True)
    incoming = incoming.reshape(3, append_len, head_size)
    lane_number = lax.axis_index("seq")
    request_id = lane_number // group_size
    cache_length = cache_lengths[request_id]
    valid_count = append_counts[request_id]
    queries = incoming[0]
    new_keys = incoming[1]
    new_values = incoming[2]
    attended = attend(queries, new_keys, new_values, kv_cache[0], cache_length, valid_count)
    position_ids = jnp.arange(append_len, dtype=jnp.int32)
    appended = jnp.concatenate([new_keys, new_values], axis=1)
    appended = jnp.where((position_ids < valid_count)[:, None], appended, jnp.zeros_like(appended))[
        None
    ]
    returned = lax.all_to_all(
        attended.reshape(seq_count, positions * head_size),
        "seq",
        split_axis=0,
        concat_axis=0,
        tiled=True,
    )
    heads_local = returned.reshape(requests, group_size, positions, head_size).transpose(0, 2, 1, 3)
    heads_local = heads_local.reshape(requests * positions, group_size * head_size)
    partial_out = jnp.dot(heads_local, w_out, preferred_element_type=jnp.float32)
    rep_index = lax.axis_index("rep")
    share_width = norm_gain.shape[0]
    summed = lax.psum(partial_out.astype(jnp.bfloat16), "rep").astype(jnp.float32)
    combined = flat_tokens.astype(jnp.float32) + summed
    mean_row = combined.sum(axis=1) / model_width
    square_row = (combined * combined).sum(axis=1) / model_width
    combined = lax.dynamic_slice_in_dim(combined, rep_index * share_width, share_width, 1)
    variance = square_row - mean_row * mean_row
    normed = (combined - mean_row[:, None]) * lax.rsqrt(variance + 1e-05)[
        :, None
    ] * norm_gain + norm_bias
    return (normed.astype(jnp.bfloat16).reshape(requests, positions, share_width), appended)


MESH = pl.DeviceIdType.MESH
NEG = -1e30
KEY_ROWS = 1024
QUERY_ROWS = 256


def fused_kernel(
    seq_count,
    lengths_ref,
    counts_ref,
    hidden_hbm,
    wq_hbm,
    wk_hbm,
    wv_hbm,
    wo_hbm,
    gain_ref,
    bias_ref,
    kv_hbm,
    out_ref,
    entries_ref,
    hid,
    wq,
    wk,
    wv,
    wo,
    keys,
    values,
    q_send,
    q_recv,
    kv_send,
    kv_recv,
    queries,
    new_values,
    ret_send,
    ret,
    heads,
    z_all,
    load_sem,
    q_ss,
    q_rs,
    kv_ss,
    kv_rs,
    wo_ss,
    wo_rs,
    ret_ss,
    ret_rs,
    pair_ss,
    pair_rs,
):
    bf16, f32 = jnp.bfloat16, jnp.float32
    lane = lax.axis_index("seq")
    rep = lax.axis_index("rep")
    far = lax.rem(rep + 2, 4)
    pair = rep + 1 - 2 * lax.rem(rep, 2)
    cross = lax.rem(pair + 2, 4)
    near_lanes = seq_count // 2
    near_base = lane // near_lanes * near_lanes
    away_base = near_lanes - near_base
    positions = hid.shape[0] // 2
    half = positions // 2
    width = hid.shape[1]
    share = wq.shape[1]
    append_len = queries.shape[0]
    cached = keys.shape[0]
    contract_last = (((1,), (1,)), ((), ()))

    def remote(src, dst, send, recv, to_seq, to_rep):
        return pltpu.make_async_remote_copy(
            src_ref=src,
            dst_ref=dst,
            send_sem=send,
            recv_sem=recv,
            device_id=(to_seq, to_rep),
            device_id_type=MESH,
        )

    loads = [
        pltpu.make_async_copy(hidden_hbm, hid, load_sem.at[0]),
        pltpu.make_async_copy(wq_hbm, wq, load_sem.at[1]),
        pltpu.make_async_copy(wk_hbm, wk, load_sem.at[2]),
        pltpu.make_async_copy(wv_hbm, wv, load_sem.at[3]),
        pltpu.make_async_copy(kv_hbm.at[0, pl.ds(0, cached)], keys, load_sem.at[4]),
        pltpu.make_async_copy(wo_hbm, wo.at[rep], load_sem.at[5]),
    ]
    for copy in loads:
        copy.start()

    barrier = pltpu.get_barrier_semaphore()
    for k in range(1, seq_count):
        pl.semaphore_signal(
            barrier, inc=1, device_id=(lax.rem(lane + k, seq_count), rep), device_id_type=MESH
        )
    for k in range(seq_count):
        pl.semaphore_signal(
            barrier, inc=1, device_id=(lax.rem(lane + k, seq_count), far), device_id_type=MESH
        )
    for k in range(near_lanes):
        for to in (pair, cross):
            pl.semaphore_signal(
                barrier,
                inc=1,
                device_id=(near_base + lax.rem(lane + k, near_lanes), to),
                device_id_type=MESH,
            )

    cut = share // 2
    wo_far, wo_pass = [], []
    for h in range(2):
        rows = pl.ds(h * cut, cut)
        wo_far.append(
            remote(wo_hbm.at[rows], wo.at[rep, rows], wo_ss.at[2 * h], wo_rs.at[2 * h], lane, far)
        )
        held = wo.at[far, rows]
        wo_pass.append(remote(held, held, wo_ss.at[2 * h + 3], wo_rs.at[2 * h + 3], lane, pair))
    wo_pair = remote(wo_hbm, wo.at[rep], wo_ss.at[1], wo_rs.at[1], lane, pair)
    pl.semaphore_wait(barrier, 3 * seq_count - 1)
    for copy in wo_far:
        copy.start()

    loads[0].wait()
    loads[1].wait()
    q_all = jnp.dot(hid[...], wq[...], preferred_element_type=f32).astype(bf16).astype(f32)
    q_all = q_all * 0.125
    for dest in range(seq_count):
        r, i = dest // 4, dest % 4
        top = q_all[r * positions : r * positions + half, i * 64 : (i + 1) * 64]
        low = q_all[r * positions + half : (r + 1) * positions, i * 64 : (i + 1) * 64]
        q_send[dest] = jnp.concatenate([top, low], axis=1).astype(bf16)

    def q_copy(k):
        to = lax.rem(lane + k, seq_count)
        return remote(q_send.at[to], q_recv.at[lane], q_ss.at[k], q_rs.at[k], to, rep)

    for k in range(1, seq_count):
        q_copy(k).start()
    q_recv[lane] = q_send[lane]

    loads[2].wait()
    loads[3].wait()
    k_all = jnp.dot(hid[...], wk[...], preferred_element_type=f32)
    v_all = jnp.dot(hid[...], wv[...], preferred_element_type=f32)
    for dest in range(seq_count):
        r, i = dest // 4, dest % 4
        rows = slice(r * positions, (r + 1) * positions)
        cols = slice(i * 64, (i + 1) * 64)
        kv_send[dest] = jnp.concatenate([k_all[rows, cols], v_all[rows, cols]], axis=1).astype(bf16)

    def kv_copy(k):
        to = lax.rem(lane + k, seq_count)
        return remote(
            kv_send.at[to],
            kv_recv.at[lane],
            kv_ss.at[k],
            kv_rs.at[k],
            to,
            rep,
        )

    for k in range(1, seq_count):
        kv_copy(k).start()
    kv_recv[lane] = kv_send[lane]

    wo_pair.start()

    request = lane // 4
    length = lengths_ref[request]
    count = counts_ref[request]
    loads[4].wait()
    first = keys[0:16, :].astype(f32)[0:1, :]
    mask_rows = 256
    lanes = lax.broadcasted_iota(jnp.int32, (mask_rows, 128), 1)
    row_ids = lax.broadcasted_iota(jnp.int32, (mask_rows, 128), 0)

    def mask_block(b, carry):
        rows = pl.ds(pl.multiple_of(b * mask_rows, mask_rows), mask_rows)
        block = keys[rows, :].astype(f32)
        keep = row_ids + b * mask_rows < length
        keys[rows, :] = jnp.where(keep, block, first).astype(bf16)
        values[rows, :] = jnp.where(keep, jnp.where(lanes < 64, 1.0, block), 0.0).astype(bf16)
        return carry

    lax.fori_loop(0, cached // mask_rows, mask_block, 0)

    for k in range(1, seq_count):
        q_copy(k).wait_recv()
    lane_half = lax.broadcasted_iota(jnp.int32, (half, 128), 1) < 64
    for s in range(seq_count):
        both = q_recv[s].astype(f32)
        queries[s * positions : s * positions + half, :] = jnp.where(lane_half, both, 0.0).astype(bf16)
        queries[s * positions + half : (s + 1) * positions, :] = jnp.where(
            lane_half, pltpu.roll(both, 64, 1), 0.0
        ).astype(bf16)

    per_chunk = QUERY_ROWS // positions
    own_chunk = lane // per_chunk
    lane_new = lax.broadcasted_iota(jnp.int32, (positions, 128), 1) < 64
    row_new = lax.broadcasted_iota(jnp.int32, (positions, 128), 0)

    def take_new_entries():
        for k in range(1, seq_count):
            kv_copy(k).wait_recv()
        for s in range(seq_count):
            block = kv_recv[s].astype(f32)
            rows = slice(s * positions, (s + 1) * positions)
            new_values[rows, :] = jnp.where(lane_new, 1.0, block).astype(bf16)
            entries_ref[rows, :] = jnp.where(
                row_new + s * positions < count, block, 0.0
            ).astype(bf16)

    to_reps = (rep, far, pair, cross)

    def ret_copy(side, s):
        return remote(
            ret_send.at[s],
            ret.at[rep, lane],
            ret_ss.at[side, s],
            ret_rs.at[side, lane],
            s,
            to_reps[side],
        )

    def wait_ret(side, s):
        remote(
            ret_send.at[s],
            ret.at[to_reps[side], s],
            ret_ss.at[side, s],
            ret_rs.at[side, s],
            s,
            to_reps[side],
        ).wait_recv()

    blocks = cached // KEY_ROWS
    def visit_chunk(step, carry):
        chunk = lax.rem(own_chunk + 1 + step, 2)
        start = pl.multiple_of(chunk * QUERY_ROWS, QUERY_ROWS)
        q = queries[pl.ds(start, QUERY_ROWS), :]

        def block_scores(b):
            if b < blocks:
                block = keys[b * KEY_ROWS : (b + 1) * KEY_ROWS, :]
                return lax.dot_general(q, block, contract_last, preferred_element_type=f32)
            fresh = kv_recv[...].reshape(append_len, 128)
            fresh = lax.dot_general(q, fresh, contract_last, preferred_element_type=f32)
            col = lax.broadcasted_iota(jnp.int32, (QUERY_ROWS, append_len), 1)
            row = lax.broadcasted_iota(jnp.int32, (QUERY_ROWS, append_len), 0) + start
            return jnp.where((col <= row) & (col < count), fresh, NEG)

        current = block_scores(0)
        top = total = None
        for b in range(blocks + 1):
            following = None
            if b < blocks:
                if b == blocks - 1:
                    pl.when(step == 0)(take_new_entries)
                following = block_scores(b + 1)
            newer = current.max(axis=1, keepdims=True)
            if b > 0:
                newer = jnp.maximum(top, newer)
            weight = jnp.exp(current - newer).astype(bf16)
            rows = values[b * KEY_ROWS : (b + 1) * KEY_ROWS, :] if b < blocks else new_values[...]
            part = jnp.dot(weight, rows, preferred_element_type=f32)
            total = part if b == 0 else total * jnp.exp(top - newer) + part
            top, current = newer, following
        attn = total / pltpu.roll(total, 64, 1)
        for t in range(per_chunk):
            upper = attn[t * positions : t * positions + half, :]
            lower = attn[t * positions + half : (t + 1) * positions, :]
            s = chunk * per_chunk + t
            ret_send[s] = jnp.where(lane_half, pltpu.roll(upper, 64, 1), lower).astype(bf16)

        @pl.when(step == 0)
        def _():
            for t in range(per_chunk):
                ret_copy(0, away_base + t).start()
                ret_copy(1, away_base + t).start()

        @pl.when(step == 1)
        def _():
            for k in range(near_lanes):
                s = near_base + lax.rem(lane + k, near_lanes)
                for side in range(4):
                    if k or side:
                        ret_copy(side, s).start()
            ret[rep, lane] = ret_send[lane]

        return carry

    lax.fori_loop(0, 2, visit_chunk, 0)

    for h in range(2):
        wo_far[h].wait_recv()
        wo_pass[h].start()

    passes = []
    for side in (0, 1):
        for k in range(near_lanes):
            wait_ret(side, away_base + k)
        away = ret.at[to_reps[side], pl.ds(away_base, near_lanes)]
        passes.append(remote(away, away, pair_ss.at[side], pair_rs.at[side], lane, pair))
        passes[side].start()
    for k in range(near_lanes):
        for side in range(4):
            if k or side:
                wait_ret(side, near_base + lax.rem(lane + k, near_lanes))

    def project(which):
        for r in range(2):
            parts = [ret[which, r * 4 + i].astype(f32) for i in range(4)]
            upper = [jnp.where(lane_half, parts[2 * g], pltpu.roll(parts[2 * g + 1], 64, 1)) for g in range(2)]
            lower = [jnp.where(lane_half, pltpu.roll(parts[2 * g], 64, 1), parts[2 * g + 1]) for g in range(2)]
            for g in range(2):
                cols = slice(g * 128, (g + 1) * 128)
                heads[r * positions : r * positions + half, cols] = upper[g].astype(bf16)
                heads[r * positions + half : (r + 1) * positions, cols] = lower[g].astype(bf16)
        part = jnp.dot(heads[...], wo[which], preferred_element_type=f32)
        return part.astype(bf16).astype(f32)

    loads[5].wait()
    z_all[...] = hid[...].astype(f32) + project(rep)
    z_all[...] += project(far)
    wo_pair.wait_recv()
    passes[0].wait_recv()
    z_all[...] += project(pair)
    for copy in wo_pass:
        copy.wait_recv()
    passes[1].wait_recv()
    z_all[...] += project(cross)
    z = z_all[...]
    mean = z.sum(axis=1, keepdims=True) / width
    square = (z * z).sum(axis=1, keepdims=True) / width
    mine = z_all[:, pl.ds(pl.multiple_of(rep * share, share), share)]
    scale = lax.rsqrt(square - mean * mean + 1e-05)
    out_ref[...] = ((mine - mean) * scale * gain_ref[...] + bias_ref[...]).astype(bf16)

    for k in range(1, seq_count):
        q_copy(k).wait_send()
        kv_copy(k).wait_send()
    for k in range(near_lanes):
        for side in range(4):
            if side < 2:
                ret_copy(side, away_base + k).wait_send()
            if k or side:
                ret_copy(side, near_base + lax.rem(lane + k, near_lanes)).wait_send()
    for copy in [wo_pair] + wo_far + wo_pass + passes:
        copy.wait_send()


def fused(
    hidden,
    w_query,
    w_key,
    w_value,
    w_out,
    norm_gain,
    norm_bias,
    kv_cache,
    cache_lengths,
    append_counts,
):
    seq_count = lax.axis_size("seq")
    requests, positions, width = hidden.shape
    share = w_query.shape[1]
    tokens = requests * positions
    append_len = positions * seq_count
    cached = kv_cache.shape[1] - append_len
    bf16, f32 = jnp.bfloat16, jnp.float32
    any_spec = pl.BlockSpec(memory_space=pltpu.HBM)
    vmem_spec = pl.BlockSpec(memory_space=pltpu.VMEM)
    smem_spec = pl.BlockSpec(memory_space=pltpu.SMEM)
    dma = pltpu.SemaphoreType.DMA
    half = positions // 2
    out, entries = pl.pallas_call(
        functools.partial(fused_kernel, seq_count),
        out_shape=(
            jax.ShapeDtypeStruct((tokens, share), bf16),
            jax.ShapeDtypeStruct((append_len, 128), bf16),
        ),
        in_specs=[smem_spec] * 2 + [any_spec] * 5 + [vmem_spec] * 2 + [any_spec],
        out_specs=(vmem_spec, vmem_spec),
        scratch_shapes=[
            pltpu.VMEM((tokens, width), bf16),
            pltpu.VMEM((width, share), bf16),
            pltpu.VMEM((width, share), bf16),
            pltpu.VMEM((width, share), bf16),
            pltpu.VMEM((4, share, width), bf16),
            pltpu.VMEM((cached, 128), bf16),
            pltpu.VMEM((cached, 128), bf16),
            pltpu.VMEM((seq_count, half, 128), bf16),
            pltpu.VMEM((seq_count, half, 128), bf16),
            pltpu.VMEM((seq_count, positions, 128), bf16),
            pltpu.VMEM((seq_count, positions, 128), bf16),
            pltpu.VMEM((append_len, 128), bf16),
            pltpu.VMEM((append_len, 128), bf16),
            pltpu.VMEM((seq_count, half, 128), bf16),
            pltpu.VMEM((4, seq_count, half, 128), bf16),
            pltpu.VMEM((tokens, share), bf16),
            pltpu.VMEM((tokens, width), f32),
            dma((6,)),
            dma((seq_count,)),
            dma((seq_count,)),
            dma((seq_count,)),
            dma((seq_count,)),
            dma((6,)),
            dma((6,)),
            dma((4, seq_count)),
            dma((4, seq_count)),
            dma((2,)),
            dma((2,)),
        ],
        compiler_params=pltpu.CompilerParams(
            collective_id=0, has_side_effects=True, vmem_limit_bytes=63 * 1024 * 1024
        ),
        name="sublayer",
    )(
        cache_lengths,
        append_counts,
        hidden.reshape(tokens, width),
        w_query,
        w_key,
        w_value,
        w_out,
        norm_gain.reshape(1, share),
        norm_bias.reshape(1, share),
        kv_cache,
    )
    return out.reshape(requests, positions, share), entries[None]


def solution(mesh):
    fits = mesh.shape["seq"] == 8 and mesh.shape["rep"] == 4
    return jax.shard_map(
        fused if fits else on_device,
        mesh=mesh,
        in_specs=(
            P(None, "seq", None),
            P(None, "rep"),
            P(None, "rep"),
            P(None, "rep"),
            P("rep", None),
            P("rep"),
            P("rep"),
            P("seq", None, "rep"),
            P(),
            P(),
        ),
        out_specs=(P(None, "seq", "rep"), P("seq", None, "rep")),
        check_vma=False,
    )
```
